512 devices in a mesh: ctx: 32 (over z_lo, x), tp: 16 (over z_hi, y, core).
Axes of the slice: x: 4, y: 4, z: 16 (z_hi: 2, z_lo: 8; z = z_hi * 8 + z_lo), core: 2. Of those that a mesh axis runs over, the one named last changes fastest.
Arguments:
- query_in: bfloat16 [16384, 4096], P('ctx', 'tp'), may hold values from -6 to 6
- key_in: bfloat16 [16384, 4096], P('ctx', 'tp'), may hold values from -6 to 6
- value_in: bfloat16 [16384, 4096], P('ctx', 'tp'), may hold values from -6 to 6
- residue: float32 [4096, 16], P('tp'), may hold values from -0.125 to 0.125
- decay_rate: float32 [4096, 16], P('tp'), may hold values from 1.8310548e-05 to 0.05
- frequency: float32 [4096, 16], P('tp'), may hold values from 0 to 0.5
- skip_gain: float32 [4096], P('tp'), may hold values from -4 to 4
- out_weight: bfloat16 [4096, 4096], P('ctx', 'tp'), may hold values from -0.1875 to 0.1875
- cotangent: bfloat16 [16384, 4096], P('ctx', 'tp'), may hold values from -6 to 6
Outputs:
- layer_out: bfloat16 [16384, 4096], P('ctx', 'tp')
- grad_query: bfloat16 [16384, 4096], P('ctx', 'tp')
- grad_key: bfloat16 [16384, 4096], P('ctx', 'tp')
- grad_value: bfloat16 [16384, 4096], P('ctx', 'tp')
The draws below stay inside these ranges and needn't reach their ends.
All inputs are finite; a program needn't handle non-finite values.
Results may differ from the reference program's by a relative error of at most 0.013.
Values may be sent and summed in bfloat16 or wider, within the bound.
A program may use at most 128 MiB of HBM per device.

```python
import math
import jax
import jax.numpy as jnp
from jax import lax

D = 4096
MODES = 16
SEQ = 16384


def raised(result, stream_key, source, target, blocks, factor):
    owner, partner = [(jnp.arange(result.shape[position]) // (result.shape[position] // blocks)).reshape([-1 if axis == position else 1 for axis in range(result.ndim)]) for position in (source, target)]
    chosen = jax.random.permutation(stream_key, blocks)[partner]
    strong = (owner == chosen) | (owner == (partner + blocks // 2) % blocks)
    return jnp.where(strong, factor * result, result)


def steps_of(rng, dims, cuts, smallest, top_value):
    def one(dim, parts):
        heights = jax.random.uniform(jax.random.fold_in(jax.random.fold_in(rng, 6), dim), (parts,), jnp.float32, smallest / len(cuts), top_value / len(cuts))
        return jnp.repeat(jnp.exp(heights), dims[dim] // parts).reshape((-1,) + (1,) * (len(dims) - dim - 1))

    gain = one(*cuts[0])
    for cut in cuts[1:]:
        gain = gain * one(*cut)
    return gain


def centred(own_key, extent, scale, limit, pieces=(), kind=jnp.bfloat16):
    gain = steps_of(own_key, extent, pieces, -0.22, 0.18) if pieces else 1.0
    array = jax.random.normal(own_key, extent, jnp.float32) * scale * gain
    return jnp.minimum(jnp.maximum(array, -limit), limit).astype(kind)


def heavy_noise(stream_key, dims, spread, reach, cuts, heavy, kind=jnp.bfloat16):
    array = spread * jax.random.normal(stream_key, dims, jnp.float32)
    if cuts:
        array = array * steps_of(stream_key, dims, cuts, -0.22, 0.18)
    return jnp.clip(raised(array, jax.random.fold_in(stream_key, 3), *heavy), -reach, reach).astype(kind)


def setup_inputs(seed: int = 0) -> dict:
    key_of = jax.random.split(jax.random.key(seed), 10)
    return {
        "query_in": centred(key_of[0], (SEQ, D), 1.0, 6.0, ((0, 32), (1, 16))),
        "key_in": centred(key_of[1], (SEQ, D), 1.0, 6.0, ((0, 32), (1, 16))),
        "value_in": centred(key_of[2], (SEQ, D), 1.0, 6.0, ((0, 32), (1, 16))),
        "residue": centred(key_of[3], (D, MODES), (1.0 / SEQ ** 0.5), 0.125, ((0, 16),), jnp.float32),
        "decay_rate": jnp.clip(jnp.exp(math.log(0.05) - 7.912301 * jax.random.uniform(key_of[4], (D, MODES), jnp.float32) ** steps_of(key_of[4], (D, MODES), ((0, 16),), -0.2, 0.2)), 1.831054760259576e-05, 0.05),
        "frequency": jnp.clip(0.5 * jax.random.uniform(key_of[5], (D, MODES), jnp.float32) ** steps_of(key_of[5], (D, MODES), ((0, 16),), -0.2, 0.2), 0.0, 0.5),
        "skip_gain": centred(key_of[6], (D,), 1.0, 4.0, ((0, 16),), jnp.float32),
        "out_weight": heavy_noise(key_of[7], (D, D), D ** -0.5, 0.1875, ((0, 32), (1, 16)), (0, 1, 32, 2.75)),
        "cotangent": centred(key_of[8], (SEQ, D), 1.0, 6.0, ((0, 32), (1, 16))),
    }


def make_filters(residue, decay_rate, frequency, length):
    positions = jnp.arange(length).astype(residue.dtype)
    scaled = decay_rate[:, :, None] * positions[None, None, :]
    turned = frequency[:, :, None] * positions[None, None, :]
    terms = residue[:, :, None] * jnp.exp(-scaled) * jnp.cos(turned)
    return jnp.sum(terms, axis=1)


def filter_block(args):
    mixed_rows, grad_rows, residue, decay_rate, frequency = args
    length = mixed_rows.shape[1]
    padded = 2 * length
    kernel = make_filters(residue, decay_rate, frequency, length)
    kernel_spec = jnp.fft.rfft(kernel, n=padded, axis=-1)
    mixed_spec = jnp.fft.rfft(mixed_rows.astype(jnp.float32), n=padded, axis=-1)
    grad_spec = jnp.fft.rfft(grad_rows.astype(jnp.float32), n=padded, axis=-1)
    conv = jnp.fft.irfft(mixed_spec * kernel_spec, n=padded, axis=-1)[:, :length]
    corr = jnp.fft.irfft(jnp.conj(kernel_spec) * grad_spec, n=padded, axis=-1)[:, :length]
    return conv.astype(jnp.bfloat16), corr.astype(jnp.bfloat16)


def reference(query_in, key_in, value_in, residue, decay_rate, frequency, skip_gain, out_weight, cotangent):
    f32 = jnp.float32
    bf16 = jnp.bfloat16
    length, width = query_in.shape
    mixed = (key_in.astype(f32) * value_in.astype(f32)).astype(bf16)
    grad_in = (cotangent.astype(f32) * query_in.astype(f32)).astype(bf16)
    block = math.gcd(width, 128)
    count = width // block
    modes = residue.shape[1]
    conv_t, corr_t = lax.map(filter_block, (
        mixed.T.reshape(count, block, length),
        grad_in.T.reshape(count, block, length),
        residue.reshape(count, block, modes),
        decay_rate.reshape(count, block, modes),
        frequency.reshape(count, block, modes)))
    conv = conv_t.reshape(width, length).T
    corr = corr_t.reshape(width, length).T
    conv, corr = lax.optimization_barrier((conv, corr))
    total = conv.astype(f32) + skip_gain[None, :] * mixed.astype(f32)
    gated = (query_in.astype(f32) * total).astype(bf16)
    grad_query = (cotangent.astype(f32) * total).astype(bf16)
    grad_mixed = corr.astype(f32) + skip_gain[None, :] * grad_in.astype(f32)
    grad_key = (grad_mixed * value_in.astype(f32)).astype(bf16)
    grad_value = (grad_mixed * key_in.astype(f32)).astype(bf16)
    layer_out = jnp.dot(gated, out_weight, preferred_element_type=f32).astype(bf16)
    return layer_out, grad_query, grad_key, grad_value
```

```python
import jax
import jax.numpy as jnp
from jax import lax
from jax.experimental import pallas as pl
from jax.experimental.pallas import tpu as pltpu
from jax.sharding import PartitionSpec as P

F32 = jnp.float32
BF16 = jnp.bfloat16
MESH = pl.DeviceIdType.MESH

NZ, NX, NY = 8, 4, 4
ROWS, LANES, HALVES = 512, 128, 2
STEP, LOS, SUBS = 16, 4, 8
STRETCH = STEP * LOS
GROUPS, PER = 4, 4
PIECES = 4
PIECE = ROWS // PIECES
FIRST, CHUNK, WIDE, DEVICE, COLUMN, GAIN = range(6)


def cmul(ar, ai, br, bi):
    return ar * br - ai * bi, ar * bi + ai * br


def shifted(value, amount, back):
    row = lax.broadcasted_iota(jnp.int32, (SUBS, LANES), 0)
    if back:
        return jnp.where(row < SUBS - amount, pltpu.roll(value, SUBS - amount, 0), 0.0)
    return jnp.where(row >= amount, pltpu.roll(value, amount, 0), 0.0)


def kernel(
    q_ref,
    k_ref,
    v_ref,
    g_ref,
    w_ref,
    par_ref,
    skip_ref,
    out_ref,
    gq_ref,
    gk_ref,
    gv_ref,
    mixed,
    grad_in,
    conv,
    partial,
    chunk_state,
    entry,
    zstate,
    powers,
    taps,
    wide_pow,
    own_state,
    recv_x,
    column,
    recv_z,
    prefix,
    entry_in,
    weights,
    gated,
    total,
    w_send_z,
    w_send_x,
    w_recv,
    s_send,
    x_recv,
    z_recv,
    p_recv,
    g_send,
    f_send,
    g_recv,
):
    ctx = lax.axis_index("ctx")
    tp = lax.axis_index("tp")
    zlo, x = lax.div(ctx, NX), lax.rem(ctx, NX)
    zhi, y, core = lax.div(tp, 2 * NY), lax.rem(lax.div(tp, 2), NY), lax.rem(tp, 2)

    def at_x(step):
        return (zlo * NX + lax.rem(x + step, NX), tp)

    def at_z(step):
        return (lax.rem(zlo + step, NZ) * NX + x, tp)

    def tp_of(h, yy, c):
        return (h * NY + yy) * 2 + c

    def at_y(step):
        return (ctx, tp_of(zhi, lax.rem(y + step, NY), core))

    far = (ctx, tp_of(1 - zhi, y, core))
    sibling = (ctx, tp_of(zhi, y, 1 - core))

    barrier = pltpu.get_barrier_semaphore()
    partners = [at_x(i) for i in range(1, NX)] + [at_z(i) for i in range(1, NZ)]
    partners += [at_y(i) for i in range(1, NY)] + [far, sibling]
    for partner in partners:
        pl.semaphore_signal(barrier, inc=1, device_id=partner, device_id_type=MESH)
    pl.semaphore_wait(barrier, len(partners))

    def copy(src, dst, send, recv, device):
        return pltpu.make_async_remote_copy(
            src_ref=src, dst_ref=dst, send_sem=send, recv_sem=recv,
            device_id=device, device_id_type=MESH,
        )

    def w_copy_z(step, right):
        block = (zlo - step if right else zlo + step) * NX + x
        slot = weights.at[block]
        to = (ctx + NX, tp) if right else (ctx - NX, tp)
        return copy(slot, slot, w_send_z.at[0 if right else 1, step], w_recv.at[block], to)

    def w_copy_x(z, step):
        block = z * NX + x
        slot = weights.at[block]
        return copy(slot, slot, w_send_x.at[z, step], w_recv.at[block], at_x(step))

    def w_wait_recv(block):
        slot = weights.at[block]
        copy(slot, slot, w_send_x.at[0, 0], w_recv.at[block], at_x(1)).wait_recv()

    def w_right(step):
        return jnp.logical_and(zlo - step >= 0, zlo < NZ - 1)

    def w_left(step):
        return jnp.logical_and(zlo + step < NZ, zlo > 0)

    def w_step(step):
        if step:
            @pl.when(zlo - step >= 0)
            def _():
                w_wait_recv((zlo - step) * NX + x)

            @pl.when(zlo + step < NZ)
            def _():
                w_wait_recv((zlo + step) * NX + x)

        @pl.when(w_right(step))
        def _():
            w_copy_z(step, True).start()

        @pl.when(w_left(step))
        def _():
            w_copy_z(step, False).start()

        @pl.when(zlo - step >= 0)
        def _():
            for i in range(1, NX):
                w_copy_x(zlo - step, i).start()

        if step:
            @pl.when(zlo + step < NZ)
            def _():
                for i in range(1, NX):
                    w_copy_x(zlo + step, i).start()

    weights[ctx] = w_ref[...]
    w_step(0)

    def make_tables(h):
        def group(mg, acc):
            one = par_ref[h, mg, FIRST]
            ar, ai = one[:PER], one[PER:]
            gain = par_ref[h, mg, GAIN][:PER]
            pr, pi = jnp.ones_like(ar), jnp.zeros_like(ai)
            acc = list(acc)
            for p in range(STEP + 1):
                powers[h, mg, p] = jnp.concatenate([pr, pi], axis=0)
                if p < STEP:
                    acc[p] = acc[p] + gain * pr
                    pr, pi = cmul(pr, pi, ar, ai)
            return tuple(acc)

        acc = lax.fori_loop(0, GROUPS, group, (jnp.zeros((PER, LANES), F32),) * STEP)
        for p in range(STEP):
            taps[h, pl.ds(p, 1)] = jnp.sum(acc[p], axis=0, keepdims=True)

    def make_wide(index, carry):
        h, mg = lax.div(index, GROUPS), lax.rem(index, GROUPS)
        row = lax.broadcasted_iota(jnp.int32, (SUBS, LANES), 0)
        for back in (False, True):
            for i in range(PER):
                start = jnp.where(row == (SUBS - 1 if back else 0), 1.0, 0.0).astype(F32)
                re, im = scan_wide(h, mg, i, start, jnp.zeros_like(start), back)
                wide_pow[int(back), h, mg, i] = re
                wide_pow[int(back), h, mg, PER + i] = im
        return carry

    def scan_wide(h, mg, i, re, im, back):
        br = par_ref[h, mg, WIDE, pl.ds(i, 1)]
        bi = par_ref[h, mg, WIDE, pl.ds(PER + i, 1)]
        for amount in (1, 2, 4):
            sr, si = cmul(br, bi, shifted(re, amount, back), shifted(im, amount, back))
            re, im = re + sr, im + si
            if amount < 4:
                br, bi = cmul(br, bi, br, bi)
        return re, im

    def rows_at(lo, b):
        return pl.ds(lo * STEP + b, SUBS, stride=STRETCH)

    def state_in(back, signal, index):
        h, mg = lax.div(index, GROUPS), lax.rem(index, GROUPS)
        way = int(back)
        acc = [[None] * LOS for _ in range(2 * PER)]
        for p in range(STEP):
            b = p if back else STEP - 1 - p
            values = [signal[h, rows_at(lo, b)] for lo in range(LOS)]
            for r in range(2 * PER):
                if p == 0:
                    for lo in range(LOS):
                        acc[r][lo] = values[lo] if r < PER else jnp.zeros_like(values[lo])
                    continue
                coef = powers[h, mg, p, pl.ds(r, 1)]
                for lo in range(LOS):
                    acc[r][lo] = acc[r][lo] + coef * values[lo]
        for i in range(PER):
            cr = par_ref[h, mg, CHUNK, pl.ds(i, 1)]
            ci = par_ref[h, mg, CHUNK, pl.ds(PER + i, 1)]
            order = list(range(LOS))[::-1] if back else list(range(LOS))
            ur, ui = acc[i][order[0]], acc[PER + i][order[0]]
            for lo in order[1:]:
                ur, ui = cmul(cr, ci, ur, ui)
                ur, ui = ur + acc[i][lo], ui + acc[PER + i][lo]
            for lo in range(LOS):
                chunk_state[way, h, mg, i, lo] = acc[i][lo]
                chunk_state[way, h, mg, PER + i, lo] = acc[PER + i][lo]
            er, ei = scan_wide(h, mg, i, shifted(ur, 1, back), shifted(ui, 1, back), back)
            entry[way, h, mg, i] = er
            entry[way, h, mg, PER + i] = ei
            br = par_ref[h, mg, WIDE, pl.ds(i, 1)]
            bi = par_ref[h, mg, WIDE, pl.ds(PER + i, 1)]
            dr, di = cmul(br, bi, er, ei)
            last = 0 if back else SUBS - 1
            own_state[mg, h, pl.ds(way * 8 + i, 1)] = (dr + ur)[last : last + 1]
            own_state[mg, h, pl.ds(way * 8 + PER + i, 1)] = (di + ui)[last : last + 1]

    def inside(back, signal, h):
        coef = [taps[h, pl.ds(p, 1)] for p in range(STEP)]
        for lo in range(LOS):
            values = [signal[h, rows_at(lo, b)] for b in range(STEP)]
            for b in range(STEP):
                js = range(b, STEP) if back else range(b + 1)
                acc = None
                for j in js:
                    term = coef[abs(b - j)] * values[j]
                    acc = term if acc is None else acc + term
                partial[int(back), h, b, lo] = acc

    def inject(back, h):
        way = int(back)

        def prepare(mg, carry):
            for i in range(PER):
                pr = entry_in[mg, h, pl.ds(way * 8 + i, 1)]
                pi = entry_in[mg, h, pl.ds(way * 8 + PER + i, 1)]
                er, ei = cmul(wide_pow[way, h, mg, i], wide_pow[way, h, mg, PER + i], pr, pi)
                zr, zi = er + entry[way, h, mg, i], ei + entry[way, h, mg, PER + i]
                cr = par_ref[h, mg, CHUNK, pl.ds(i, 1)]
                ci = par_ref[h, mg, CHUNK, pl.ds(PER + i, 1)]
                gain = par_ref[h, mg, GAIN, pl.ds(i, 1)]
                order = list(range(LOS))[::-1] if back else list(range(LOS))
                for n, lo in enumerate(order):
                    zstate[mg, i, lo] = gain * zr
                    zstate[mg, PER + i, lo] = -(gain * zi)
                    if n < LOS - 1:
                        zr, zi = cmul(cr, ci, zr, zi)
                        zr = zr + chunk_state[way, h, mg, i, lo]
                        zi = zi + chunk_state[way, h, mg, PER + i, lo]
            return carry

        lax.fori_loop(0, GROUPS, prepare, 0)
        for b0 in range(0, STEP, 4):

            def group(mg, acc):
                acc = list(acc)
                for r in range(2 * PER):
                    states = [zstate[mg, r, lo] for lo in range(LOS)]
                    for n in range(4):
                        b = b0 + n
                        coef = powers[h, mg, STEP - b if back else b + 1, pl.ds(r, 1)]
                        for lo in range(LOS):
                            acc[n * LOS + lo] = acc[n * LOS + lo] + coef * states[lo]
                return tuple(acc)

            start = tuple(partial[way, h, b0 + n, lo] for n in range(4) for lo in range(LOS))
            acc = lax.fori_loop(0, GROUPS, group, start)
            for n in range(4):
                for lo in range(LOS):
                    conv[h, rows_at(lo, b0 + n)] = acc[n * LOS + lo]

    def lanes(h):
        return pl.ds(h * LANES, LANES)

    def prepare_rows(h):
        for r0 in range(0, ROWS, 128):
            rows = pl.ds(r0, 128)
            prod = k_ref[rows, lanes(h)].astype(F32) * v_ref[rows, lanes(h)].astype(F32)
            mixed[h, rows] = prod.astype(BF16).astype(F32)
            prod = g_ref[rows, lanes(h)].astype(F32) * q_ref[rows, lanes(h)].astype(F32)
            grad_in[h, rows] = prod.astype(BF16).astype(F32)

    def gate_forward(h):
        skip = skip_ref[:, lanes(h)]
        for r0 in range(0, ROWS, 128):
            rows = pl.ds(r0, 128)
            summed = conv[h, rows].astype(BF16).astype(F32) + skip * mixed[h, rows]
            gated[tp, h, rows] = (q_ref[rows, lanes(h)].astype(F32) * summed).astype(BF16)
            gq_ref[rows, lanes(h)] = (g_ref[rows, lanes(h)].astype(F32) * summed).astype(BF16)

    def gate_backward(h):
        skip = skip_ref[:, lanes(h)]
        for r0 in range(0, ROWS, 128):
            rows = pl.ds(r0, 128)
            summed = conv[h, rows].astype(BF16).astype(F32) + skip * grad_in[h, rows]
            gk_ref[rows, lanes(h)] = (summed * v_ref[rows, lanes(h)].astype(F32)).astype(BF16)
            gv_ref[rows, lanes(h)] = (summed * k_ref[rows, lanes(h)].astype(F32)).astype(BF16)

    for h in range(HALVES):
        make_tables(h)
        prepare_rows(h)

    def forward_states(index, carry):
        state_in(False, mixed, index)
        return carry

    def backward_states(index, carry):
        state_in(True, grad_in, index)
        return carry

    lax.fori_loop(0, HALVES * GROUPS, forward_states, 0)
    lax.fori_loop(0, HALVES * GROUPS, backward_states, 0)
    lax.fori_loop(0, HALVES * GROUPS, make_wide, 0)

    round_x = [
        copy(own_state.at[lax.rem(x + i, NX)], recv_x.at[x], s_send.at[0, i], x_recv.at[x], at_x(i))
        for i in range(1, NX)
    ]
    for c in round_x:
        c.start()
    recv_x[x] = own_state[x]
    w_step(1)
    inside(False, mixed, 0)
    for i in range(1, NX):
        src = lax.rem(x + NX - i, NX)
        copy(own_state.at[0], recv_x.at[src], s_send.at[0, i], x_recv.at[src], at_x(i)).wait_recv()

    def cpack(value):
        return value[:PER], value[PER:]

    def step_on(power, h, state, added):
        re, im = cmul(*cpack(par_ref[h, x, power]), *cpack(state))
        return jnp.concatenate([re, im], axis=0) + added

    for h in range(HALVES):
        state = recv_x[0, h, pl.ds(0, 8)]
        for i in range(1, NX):
            state = step_on(DEVICE, h, state, recv_x[i, h, pl.ds(0, 8)])
        column[0, h] = state
        state = recv_x[NX - 1, h, pl.ds(8, 8)]
        for i in range(NX - 2, -1, -1):
            state = step_on(DEVICE, h, state, recv_x[i, h, pl.ds(8, 8)])
        column[1, h] = state

    round_z = []
    for i in range(1, NZ):
        way = jnp.where(zlo + i < NZ, 0, 1)
        round_z.append(
            copy(column.at[way], recv_z.at[zlo], s_send.at[1, i], z_recv.at[zlo], at_z(i))
        )
    for c in round_z:
        c.start()
    recv_z[zlo] = jnp.zeros_like(recv_z[zlo])
    inside(False, mixed, 1)
    w_step(2)
    inside(True, grad_in, 0)
    inside(True, grad_in, 1)
    for i in range(1, NZ):
        src = lax.rem(zlo + NZ - i, NZ)
        copy(column.at[0], recv_z.at[src], s_send.at[1, i], z_recv.at[src], at_z(i)).wait_recv()

    for h in range(HALVES):
        state = jnp.zeros((2 * PER, LANES), F32)
        for z in range(NZ):
            state = jnp.where(z < zlo, step_on(COLUMN, h, state, recv_z[z, h]), state)
        for i in range(NX):
            prefix[i, h, pl.ds(0, 8)] = state
            if i < NX - 1:
                state = step_on(DEVICE, h, state, recv_x[i, h, pl.ds(0, 8)])
        state = jnp.zeros((2 * PER, LANES), F32)
        for z in range(NZ - 1, -1, -1):
            state = jnp.where(z > zlo, step_on(COLUMN, h, state, recv_z[z, h]), state)
        for i in range(NX - 1, -1, -1):
            prefix[i, h, pl.ds(8, 8)] = state
            if i > 0:
                state = step_on(DEVICE, h, state, recv_x[i, h, pl.ds(8, 8)])

    round_p = [
        copy(prefix.at[lax.rem(x + i, NX)], entry_in.at[x], s_send.at[2, i], p_recv.at[x], at_x(i))
        for i in range(1, NX)
    ]
    for c in round_p:
        c.start()
    entry_in[x] = prefix[x]
    w_step(3)
    for i in range(1, NX):
        src = lax.rem(x + NX - i, NX)
        copy(prefix.at[0], entry_in.at[src], s_send.at[2, i], p_recv.at[src], at_x(i)).wait_recv()

    def piece(block, h, n):
        return gated.at[block, h, pl.ds(n * PIECE, PIECE)]

    def half(block, h):
        return gated.at[block, h]

    sends = []

    def send(src, sem, recv, to):
        c = copy(src, src, sem, recv, to)
        c.start()
        sends.append(c)

    for h in range(HALVES):
        inject(False, h)
        gate_forward(h)
        for n in range(PIECES):
            send(piece(tp, h, n), g_send.at[h, n], g_recv.at[tp, h, n], far)
        for i in range(1, NY):
            send(half(tp, h), g_send.at[h, PIECES + i - 1], g_recv.at[tp, h, 0], at_y(i))
        send(half(tp, h), g_send.at[h, PIECES + 3], g_recv.at[tp, h, 0], sibling)
        w_step(4 + h)

    for h in range(HALVES):
        inject(True, h)
        gate_backward(h)
        if h == 0:
            w_step(6)
    w_step(7)

    far_tp = far[1]

    def wait_half(block, h):
        copy(half(block, h), half(block, h), g_send.at[0, 0], g_recv.at[block, h, 0], far).wait_recv()

    def wait_piece(block, h, n):
        part = piece(block, h, n)
        copy(part, part, g_send.at[0, 0], g_recv.at[block, h, n], far).wait_recv()

    for h in range(HALVES):
        for i in range(1, NY):
            block = tp_of(zhi, lax.rem(y + NY - i, NY), core)
            wait_half(block, h)
            send(half(block, h), f_send.at[0, h, i], g_recv.at[block, h, 0], sibling)

    def pass_on(h, n):
        wait_piece(far_tp, h, n)
        for i in range(1, NY):
            to = at_y(i)
            send(piece(far_tp, h, n), f_send.at[1 + n, h, i], g_recv.at[far_tp, h, n], to)
        send(piece(far_tp, h, n), f_send.at[1 + n, h, 0], g_recv.at[far_tp, h, n], sibling)

    def pass_core(h, n):
        for i in range(1, NY):
            block = tp_of(1 - zhi, lax.rem(y + NY - i, NY), core)
            wait_piece(block, h, n)
            send(
                piece(block, h, n), f_send.at[1 + PIECES + n, h, i], g_recv.at[block, h, n], sibling
            )

    def near_product():
        for h in range(HALVES):
            for i in range(NY):
                wait_half(tp_of(zhi, i, 1 - core), h)

        for z in range(NZ):
            for i in range(1, NX):
                w_wait_recv(z * NX + lax.rem(x + i, NX))

        def rows_of(n, carry):
            rows = pl.ds(pl.multiple_of(n * PIECE, PIECE), PIECE)
            left = jnp.concatenate(
                [gated[zhi * 8 + j, h, rows] for j in range(8) for h in range(HALVES)], axis=1
            )
            right = jnp.concatenate([weights[zhi * 16 + j] for j in range(16)], axis=0)
            total[rows] = jnp.dot(left, right, preferred_element_type=F32)
            return carry

        lax.fori_loop(0, PIECES, rows_of, 0)

    def far_product(h, n):
        for i in range(NY):
            wait_piece(tp_of(1 - zhi, i, 1 - core), h, n)
        first = (1 - zhi) * 8
        rows = pl.ds(n * PIECE, PIECE)
        left = jnp.concatenate([gated[first + j, h, rows] for j in range(8)], axis=1)
        right = jnp.concatenate([weights[2 * (first + j) + h] for j in range(8)], axis=0)
        summed = total[rows] + jnp.dot(left, right, preferred_element_type=F32)
        if h == HALVES - 1:
            out_ref[rows] = summed.astype(BF16)
        else:
            total[rows] = summed

    order = [(h, n) for h in range(HALVES) for n in range(PIECES)]
    near_at = 5
    for s in range(len(order) + 2):
        if s < len(order):
            pass_on(*order[s])
        if s == near_at:
            near_product()
            for t in range(s - 1):
                far_product(*order[t])
        if 1 <= s <= len(order):
            pass_core(*order[s - 1])
        if s > near_at:
            far_product(*order[s - 2])

    for c in sends + round_x + round_z + round_p:
        c.wait_send()
    for step in range(NZ):
        @pl.when(w_right(step))
        def _():
            w_copy_z(step, True).wait_send()

        @pl.when(w_left(step))
        def _():
            w_copy_z(step, False).wait_send()

    for z in range(NZ):
        for i in range(1, NX):
            w_copy_x(z, i).wait_send()


def body(
    query_in, key_in, value_in, residue, decay_rate, frequency, skip_gain, out_weight, cotangent
):
    def arranged(array):
        return array.reshape(HALVES, LANES, GROUPS, PER).transpose(0, 2, 3, 1)

    decay, freq = arranged(decay_rate), arranged(frequency)
    count = jnp.array([1.0, STEP, STRETCH, ROWS, ROWS * NX], F32).reshape(5, 1, 1)
    size = jnp.exp(-(decay[:, :, None] * count))
    angle = freq[:, :, None] * count
    table = jnp.concatenate([size * jnp.cos(angle), size * jnp.sin(angle)], axis=3)
    gain = jnp.concatenate([arranged(residue)] * 2, axis=2)[:, :, None]
    params = jnp.concatenate([table, gain], axis=2)

    vmem = pl.BlockSpec(memory_space=pltpu.VMEM)
    stream = jax.ShapeDtypeStruct((ROWS, HALVES * LANES), BF16)
    blocks = lax.axis_size("tp")
    sem = pltpu.SemaphoreType.DMA
    tile = (SUBS, LANES)
    return pl.pallas_call(
        kernel,
        out_shape=(stream,) * 4,
        in_specs=[vmem] * 7,
        out_specs=(vmem,) * 4,
        scratch_shapes=[
            pltpu.VMEM((HALVES, ROWS, LANES), F32),
            pltpu.VMEM((HALVES, ROWS, LANES), F32),
            pltpu.VMEM((HALVES, ROWS, LANES), F32),
            pltpu.VMEM((2, HALVES, STEP, LOS) + tile, F32),
            pltpu.VMEM((2, HALVES, GROUPS, 2 * PER, LOS) + tile, F32),
            pltpu.VMEM((2, HALVES, GROUPS, 2 * PER) + tile, F32),
            pltpu.VMEM((GROUPS, 2 * PER, LOS) + tile, F32),
            pltpu.VMEM((HALVES, GROUPS, STEP + 1, 2 * PER, LANES), F32),
            pltpu.VMEM((HALVES, STEP, LANES), F32),
            pltpu.VMEM((2, HALVES, GROUPS, 2 * PER) + tile, F32),
            pltpu.VMEM((GROUPS, HALVES, 4 * PER, LANES), F32),
            pltpu.VMEM((NX, HALVES, 4 * PER, LANES), F32),
            pltpu.VMEM((2, HALVES, 2 * PER, LANES), F32),
            pltpu.VMEM((NZ, HALVES, 2 * PER, LANES), F32),
            pltpu.VMEM((NX, HALVES, 4 * PER, LANES), F32),
            pltpu.VMEM((GROUPS, HALVES, 4 * PER, LANES), F32),
            pltpu.VMEM((NZ * NX, 128, HALVES * LANES), BF16),
            pltpu.VMEM((blocks, HALVES, ROWS, LANES), BF16),
            pltpu.VMEM((ROWS, HALVES * LANES), F32),
            sem((2, NZ)),
            sem((NZ, NX)),
            sem((NZ * NX,)),
            sem((3, NZ)),
            sem((NX,)),
            sem((NZ,)),
            sem((NX,)),
            sem((HALVES, PIECES + 4)),
            sem((1 + 2 * PIECES, HALVES, 4)),
            sem((blocks, HALVES, PIECES)),
        ],
        compiler_params=pltpu.CompilerParams(
            collective_id=0, has_side_effects=True, vmem_limit_bytes=48 * 1024 * 1024
        ),
    )(query_in, key_in, value_in, cotangent, out_weight, params, skip_gain.reshape(1, -1))


def solution(mesh):
    return jax.shard_map(
        body,
        mesh=mesh,
        in_specs=(
            P("ctx", "tp"),
            P("ctx", "tp"),
            P("ctx", "tp"),
            P("tp", None),
            P("tp", None),
            P("tp", None),
            P("tp"),
            P("ctx", "tp"),
            P("ctx", "tp"),
        ),
        out_specs=(P("ctx", "tp"), P("ctx", "tp"), P("ctx", "tp"), P("ctx", "tp")),
        check_vma=False,
    )
```

```python
import jax
import jax.numpy as jnp
from jax import lax
from jax.experimental import pallas as pl
from jax.experimental.pallas import tpu as pltpu
from jax.sharding import PartitionSpec as P

F32 = jnp.float32
BF16 = jnp.bfloat16
MESH = pl.DeviceIdType.MESH

NZ, NX, NY = 8, 4, 4
ROWS, LANES, HALVES = 512, 128, 2
STEP, LOS, SUBS = 16, 4, 8
STRETCH = STEP * LOS
GROUPS, PER = 4, 4
PIECES = 2
PIECE = ROWS // PIECES
HOPS = ((0, 1), (0, 4), (1, 1), (2, 1), (4, 1), (4, 2), (4, 3))
FIRST, CHUNK, WIDE, DEVICE, COLUMN, GAIN = range(6)


def cmul(ar, ai, br, bi):
    return ar * br - ai * bi, ar * bi + ai * br


def shifted(value, amount, back):
    row = lax.broadcasted_iota(jnp.int32, (SUBS, LANES), 0)
    if back:
        return jnp.where(row < SUBS - amount, pltpu.roll(value, SUBS - amount, 0), 0.0)
    return jnp.where(row >= amount, pltpu.roll(value, amount, 0), 0.0)


def kernel(
    q_hbm,
    k_hbm,
    v_hbm,
    g_hbm,
    w_hbm,
    par_ref,
    skip_ref,
    out_ref,
    gq_ref,
    gk_ref,
    gv_ref,
    q_ref,
    k_ref,
    v_ref,
    g_ref,
    mixed,
    grad_in,
    conv,
    partial,
    chunk_state,
    entry,
    zstate,
    powers,
    taps,
    wide_pow,
    own_state,
    recv_x,
    column,
    recv_z,
    prefix,
    entry_in,
    weights,
    gated,
    total,
    in_sem,
    w_send_z,
    w_send_x,
    w_recv,
    s_send,
    x_recv,
    z_recv,
    p_recv,
    g_send,
    f_send,
    g_recv,
    c_recv,
):
    ctx = lax.axis_index("ctx")
    tp = lax.axis_index("tp")
    zlo, x = lax.div(ctx, NX), lax.rem(ctx, NX)
    zhi, y, core = lax.div(tp, 2 * NY), lax.rem(lax.div(tp, 2), NY), lax.rem(tp, 2)

    loads = [
        pltpu.make_async_copy(src, dst, in_sem.at[n])
        for n, (src, dst) in enumerate(
            [(k_hbm, k_ref), (v_hbm, v_ref), (q_hbm, q_ref), (g_hbm, g_ref)]
            + [(w_hbm, weights.at[ctx])]
        )
    ]
    for load in loads:
        load.start()

    def at_x(step):
        return (zlo * NX + lax.rem(x + step, NX), tp)

    def at_z(step):
        return (lax.rem(zlo + step, NZ) * NX + x, tp)

    def tp_of(h, yy, c):
        return (h * NY + yy) * 2 + c

    def at_y(step):
        return (ctx, tp_of(zhi, lax.rem(y + step, NY), core))

    far = (ctx, tp_of(1 - zhi, y, core))
    sibling = (ctx, tp_of(zhi, y, 1 - core))

    barrier = pltpu.get_barrier_semaphore()
    partners = [at_x(i) for i in range(1, NX)] + [at_z(i) for i in range(1, NZ)]
    partners += [at_y(i) for i in range(1, NY)] + [far, sibling]
    for partner in partners:
        pl.semaphore_signal(barrier, inc=1, device_id=partner, device_id_type=MESH)

    def copy(src, dst, send, recv, device):
        return pltpu.make_async_remote_copy(
            src_ref=src, dst_ref=dst, send_sem=send, recv_sem=recv,
            device_id=device, device_id_type=MESH,
        )

    def w_copy_z(n, right):
        away, hop = HOPS[n]
        block = (zlo - away if right else zlo + away) * NX + x
        slot = weights.at[block]
        to = (ctx + hop * NX, tp) if right else (ctx - hop * NX, tp)
        return copy(slot, slot, w_send_z.at[0 if right else 1, n], w_recv.at[block], to)

    def w_copy_x(z, step):
        block = z * NX + x
        slot = weights.at[block]
        return copy(slot, slot, w_send_x.at[z, step], w_recv.at[block], at_x(step))

    def w_wait_recv(block):
        slot = weights.at[block]
        copy(slot, slot, w_send_x.at[0, 0], w_recv.at[block], at_x(1)).wait_recv()

    def w_right(n):
        away, hop = HOPS[n]
        return jnp.logical_and(zlo - away >= 0, zlo + hop < NZ)

    def w_left(n):
        away, hop = HOPS[n]
        return jnp.logical_and(zlo + away < NZ, zlo - hop >= 0)

    def w_arrived(step):
        @pl.when(zlo - step >= 0)
        def _():
            w_wait_recv((zlo - step) * NX + x)

        @pl.when(zlo + step < NZ)
        def _():
            w_wait_recv((zlo + step) * NX + x)

    def w_step(*which):
        for n in which:
            @pl.when(w_right(n))
            def _():
                w_copy_z(n, True).start()

            @pl.when(w_left(n))
            def _():
                w_copy_z(n, False).start()

    def w_spread(step):
        @pl.when(zlo - step >= 0)
        def _():
            for i in range(1, NX):
                w_copy_x(zlo - step, i).start()

        if step:
            @pl.when(zlo + step < NZ)
            def _():
                for i in range(1, NX):
                    w_copy_x(zlo + step, i).start()

    def make_tables(h):
        def group(mg, acc):
            one = par_ref[h, mg, FIRST]
            ar, ai = one[:PER], one[PER:]
            gain = par_ref[h, mg, GAIN][:PER]
            pr, pi = jnp.ones_like(ar), jnp.zeros_like(ai)
            acc = list(acc)
            for p in range(STEP + 1):
                powers[h, mg, p] = jnp.concatenate([pr, pi], axis=0)
                if p < STEP:
                    acc[p] = acc[p] + gain * pr
                    pr, pi = cmul(pr, pi, ar, ai)
            return tuple(acc)

        acc = lax.fori_loop(0, GROUPS, group, (jnp.zeros((PER, LANES), F32),) * STEP)
        for p in range(STEP):
            taps[h, pl.ds(p, 1)] = jnp.sum(acc[p], axis=0, keepdims=True)

    def make_wide(index, carry):
        h, mg = lax.div(index, GROUPS), lax.rem(index, GROUPS)
        row = lax.broadcasted_iota(jnp.int32, (SUBS, LANES), 0)
        for back in (False, True):
            for i in range(PER):
                start = jnp.where(row == (SUBS - 1 if back else 0), 1.0, 0.0).astype(F32)
                re, im = scan_wide(h, mg, i, start, jnp.zeros_like(start), back)
                wide_pow[int(back), h, mg, i] = re
                wide_pow[int(back), h, mg, PER + i] = im
        return carry

    def scan_wide(h, mg, i, re, im, back):
        br = par_ref[h, mg, WIDE, pl.ds(i, 1)]
        bi = par_ref[h, mg, WIDE, pl.ds(PER + i, 1)]
        for amount in (1, 2, 4):
            sr, si = cmul(br, bi, shifted(re, amount, back), shifted(im, amount, back))
            re, im = re + sr, im + si
            if amount < 4:
                br, bi = cmul(br, bi, br, bi)
        return re, im

    def rows_at(lo, b):
        return pl.ds(lo * STEP + b, SUBS, stride=STRETCH)

    def state_in(back, signal, index):
        h, mg = lax.div(index, GROUPS), lax.rem(index, GROUPS)
        way = int(back)
        acc = [[None] * LOS for _ in range(2 * PER)]
        for p in range(STEP):
            b = p if back else STEP - 1 - p
            values = [signal[h, rows_at(lo, b)] for lo in range(LOS)]
            for r in range(2 * PER):
                if p == 0:
                    for lo in range(LOS):
                        acc[r][lo] = values[lo] if r < PER else jnp.zeros_like(values[lo])
                    continue
                coef = powers[h, mg, p, pl.ds(r, 1)]
                for lo in range(LOS):
                    acc[r][lo] = acc[r][lo] + coef * values[lo]
        for i in range(PER):
            cr = par_ref[h, mg, CHUNK, pl.ds(i, 1)]
            ci = par_ref[h, mg, CHUNK, pl.ds(PER + i, 1)]
            order = list(range(LOS))[::-1] if back else list(range(LOS))
            ur, ui = acc[i][order[0]], acc[PER + i][order[0]]
            for lo in order[1:]:
                ur, ui = cmul(cr, ci, ur, ui)
                ur, ui = ur + acc[i][lo], ui + acc[PER + i][lo]
            for lo in range(LOS):
                chunk_state[way, h, mg, i, lo] = acc[i][lo]
                chunk_state[way, h, mg, PER + i, lo] = acc[PER + i][lo]
            er, ei = scan_wide(h, mg, i, shifted(ur, 1, back), shifted(ui, 1, back), back)
            entry[way, h, mg, i] = er
            entry[way, h, mg, PER + i] = ei
            br = par_ref[h, mg, WIDE, pl.ds(i, 1)]
            bi = par_ref[h, mg, WIDE, pl.ds(PER + i, 1)]
            dr, di = cmul(br, bi, er, ei)
            last = 0 if back else SUBS - 1
            own_state[mg, h, pl.ds(way * 8 + i, 1)] = (dr + ur)[last : last + 1]
            own_state[mg, h, pl.ds(way * 8 + PER + i, 1)] = (di + ui)[last : last + 1]

    def inside(back, signal, h):
        coef = [taps[h, pl.ds(p, 1)] for p in range(STEP)]
        for lo in range(LOS):
            values = [signal[h, rows_at(lo, b)] for b in range(STEP)]
            for b in range(STEP):
                js = range(b, STEP) if back else range(b + 1)
                acc = None
                for j in js:
                    term = coef[abs(b - j)] * values[j]
                    acc = term if acc is None else acc + term
                partial[int(back), h, b, lo] = acc

    def inject(back, h):
        way = int(back)

        def prepare(mg, carry):
            for i in range(PER):
                pr = entry_in[mg, h, pl.ds(way * 8 + i, 1)]
                pi = entry_in[mg, h, pl.ds(way * 8 + PER + i, 1)]
                er, ei = cmul(wide_pow[way, h, mg, i], wide_pow[way, h, mg, PER + i], pr, pi)
                zr, zi = er + entry[way, h, mg, i], ei + entry[way, h, mg, PER + i]
                cr = par_ref[h, mg, CHUNK, pl.ds(i, 1)]
                ci = par_ref[h, mg, CHUNK, pl.ds(PER + i, 1)]
                gain = par_ref[h, mg, GAIN, pl.ds(i, 1)]
                order = list(range(LOS))[::-1] if back else list(range(LOS))
                for n, lo in enumerate(order):
                    zstate[mg, i, lo] = gain * zr
                    zstate[mg, PER + i, lo] = -(gain * zi)
                    if n < LOS - 1:
                        zr, zi = cmul(cr, ci, zr, zi)
                        zr = zr + chunk_state[way, h, mg, i, lo]
                        zi = zi + chunk_state[way, h, mg, PER + i, lo]
            return carry

        lax.fori_loop(0, GROUPS, prepare, 0)
        for b0 in range(0, STEP, 4):

            def group(mg, acc):
                acc = list(acc)
                for r in range(2 * PER):
                    states = [zstate[mg, r, lo] for lo in range(LOS)]
                    for n in range(4):
                        b = b0 + n
                        coef = powers[h, mg, STEP - b if back else b + 1, pl.ds(r, 1)]
                        for lo in range(LOS):
                            acc[n * LOS + lo] = acc[n * LOS + lo] + coef * states[lo]
                return tuple(acc)

            start = tuple(partial[way, h, b0 + n, lo] for n in range(4) for lo in range(LOS))
            acc = lax.fori_loop(0, GROUPS, group, start)
            for n in range(4):
                for lo in range(LOS):
                    conv[h, rows_at(lo, b0 + n)] = acc[n * LOS + lo]

    def lanes(h):
        return pl.ds(h * LANES, LANES)

    def prepare_rows(h):
        for r0 in range(0, ROWS, 128):
            rows = pl.ds(r0, 128)
            prod = k_ref[rows, lanes(h)].astype(F32) * v_ref[rows, lanes(h)].astype(F32)
            mixed[h, rows] = prod.astype(BF16).astype(F32)
            prod = g_ref[rows, lanes(h)].astype(F32) * q_ref[rows, lanes(h)].astype(F32)
            grad_in[h, rows] = prod.astype(BF16).astype(F32)

    def gate_forward(h):
        skip = skip_ref[:, lanes(h)]
        for r0 in range(0, ROWS, 128):
            rows = pl.ds(r0, 128)
            summed = conv[h, rows].astype(BF16).astype(F32) + skip * mixed[h, rows]
            gated[zhi, core, y, h, rows] = (q_ref[rows, lanes(h)].astype(F32) * summed).astype(BF16)
            gq_ref[rows, lanes(h)] = (g_ref[rows, lanes(h)].astype(F32) * summed).astype(BF16)

    def gate_backward(h):
        skip = skip_ref[:, lanes(h)]
        for r0 in range(0, ROWS, 128):
            rows = pl.ds(r0, 128)
            summed = conv[h, rows].astype(BF16).astype(F32) + skip * grad_in[h, rows]
            gk_ref[rows, lanes(h)] = (summed * v_ref[rows, lanes(h)].astype(F32)).astype(BF16)
            gv_ref[rows, lanes(h)] = (summed * k_ref[rows, lanes(h)].astype(F32)).astype(BF16)

    for h in range(HALVES):
        make_tables(h)
    for load in loads[:-1]:
        load.wait()
    for h in range(HALVES):
        prepare_rows(h)

    def forward_states(index, carry):
        state_in(False, mixed, index)
        return carry

    def backward_states(index, carry):
        state_in(True, grad_in, index)
        return carry

    lax.fori_loop(0, HALVES * GROUPS, forward_states, 0)
    lax.fori_loop(0, HALVES * GROUPS, backward_states, 0)
    lax.fori_loop(0, HALVES * GROUPS, make_wide, 0)
    for h in range(HALVES):
        inside(False, mixed, h)
        inside(True, grad_in, h)
    loads[-1].wait()
    pl.semaphore_wait(barrier, len(partners))

    round_x = [
        copy(own_state.at[lax.rem(x + i, NX)], recv_x.at[x], s_send.at[0, i], x_recv.at[x], at_x(i))
        for i in range(1, NX)
    ]
    for c in round_x:
        c.start()
    recv_x[x] = own_state[x]
    w_step(0, 1)
    for i in range(1, NX):
        src = lax.rem(x + NX - i, NX)
        copy(own_state.at[0], recv_x.at[src], s_send.at[0, i], x_recv.at[src], at_x(i)).wait_recv()

    def cpack(value):
        return value[:PER], value[PER:]

    def step_on(power, h, state, added):
        re, im = cmul(*cpack(par_ref[h, x, power]), *cpack(state))
        return jnp.concatenate([re, im], axis=0) + added

    for h in range(HALVES):
        state = recv_x[0, h, pl.ds(0, 8)]
        for i in range(1, NX):
            state = step_on(DEVICE, h, state, recv_x[i, h, pl.ds(0, 8)])
        column[0, h] = state
        state = recv_x[NX - 1, h, pl.ds(8, 8)]
        for i in range(NX - 2, -1, -1):
            state = step_on(DEVICE, h, state, recv_x[i, h, pl.ds(8, 8)])
        column[1, h] = state

    round_z = []
    for i in range(1, NZ):
        way = jnp.where(zlo + i < NZ, 0, 1)
        round_z.append(
            copy(column.at[way], recv_z.at[zlo], s_send.at[1, i], z_recv.at[zlo], at_z(i))
        )
    for c in round_z:
        c.start()
    recv_z[zlo] = jnp.zeros_like(recv_z[zlo])
    w_spread(0)
    w_arrived(1)
    w_step(2)
    for i in range(1, NZ):
        src = lax.rem(zlo + NZ - i, NZ)
        copy(column.at[0], recv_z.at[src], s_send.at[1, i], z_recv.at[src], at_z(i)).wait_recv()

    for h in range(HALVES):
        state = jnp.zeros((2 * PER, LANES), F32)
        for z in range(NZ):
            state = jnp.where(z < zlo, step_on(COLUMN, h, state, recv_z[z, h]), state)
        for i in range(NX):
            prefix[i, h, pl.ds(0, 8)] = state
            if i < NX - 1:
                state = step_on(DEVICE, h, state, recv_x[i, h, pl.ds(0, 8)])
        state = jnp.zeros((2 * PER, LANES), F32)
        for z in range(NZ - 1, -1, -1):
            state = jnp.where(z > zlo, step_on(COLUMN, h, state, recv_z[z, h]), state)
        for i in range(NX - 1, -1, -1):
            prefix[i, h, pl.ds(8, 8)] = state
            if i > 0:
                state = step_on(DEVICE, h, state, recv_x[i, h, pl.ds(8, 8)])

    round_p = [
        copy(prefix.at[lax.rem(x + i, NX)], entry_in.at[x], s_send.at[2, i], p_recv.at[x], at_x(i))
        for i in range(1, NX)
    ]
    for c in round_p:
        c.start()
    entry_in[x] = prefix[x]
    w_arrived(2)
    w_arrived(4)
    w_step(3, 4, 5, 6)
    for i in range(1, NX):
        src = lax.rem(x + NX - i, NX)
        copy(prefix.at[0], entry_in.at[src], s_send.at[2, i], p_recv.at[src], at_x(i)).wait_recv()

    def piece(side, yy, h, n):
        return gated.at[side, core, yy, h, pl.ds(n * PIECE, PIECE)]

    def half(side, yy, h):
        return gated.at[side, core, yy, h]

    sends = []

    def send(src, sem, recv, to):
        c = copy(src, src, sem, recv, to)
        c.start()
        sends.append(c)

    def send_far(h, n):
        send(piece(zhi, y, h, n), g_send.at[h, n], g_recv.at[zhi, y, h, n], far)

    for h in range(HALVES):
        inject(False, h)
        gate_forward(h)
        for n in range(PIECES):
            send_far(h, n)
        for i in range(1, NY):
            send(half(zhi, y, h), g_send.at[h, PIECES + i - 1], g_recv.at[zhi, y, h, 0], at_y(i))
        w_spread(1 + h)

    for h in range(HALVES):
        inject(True, h)
        gate_backward(h)
        w_spread(4 - h)
        if h == 0:
            w_arrived(3)
    for step in range(5, NZ):
        w_arrived(step)
        w_spread(step)

    other = 1 - zhi

    def arrived(part, recv):
        copy(part, part, g_send.at[0, 0], recv, far).wait_recv()

    for h in range(HALVES):
        for i in range(1, NY):
            yy = lax.rem(y + i, NY)
            arrived(half(zhi, yy, h), g_recv.at[zhi, yy, h, 0])
        send(gated.at[zhi, core, :, h], f_send.at[0, h, 0], c_recv.at[0, h, 0], sibling)

    def pass_on(h, n):
        part = piece(other, y, h, n)
        arrived(part, g_recv.at[other, y, h, n])
        for i in range(1, NY):
            send(part, f_send.at[1 + n, h, i], g_recv.at[other, y, h, n], at_y(i))

    def along_y(h, n):
        return gated.at[other, core, :, h, pl.ds(n * PIECE, PIECE)]

    def pass_core(h, n):
        for i in range(1, NY):
            yy = lax.rem(y + i, NY)
            arrived(piece(other, yy, h, n), g_recv.at[other, yy, h, n])
        send(along_y(h, n), f_send.at[1 + n, h, 0], c_recv.at[1, h, n], sibling)

    def near_product():
        for h in range(HALVES):
            arrived(gated.at[zhi, 1 - core, :, h], c_recv.at[0, h, 0])

        for z in range(NZ):
            for i in range(1, NX):
                w_wait_recv(z * NX + lax.rem(x + i, NX))

        def rows_of(n, carry):
            rows = pl.ds(pl.multiple_of(n * 256, 256), 256)
            left = jnp.concatenate(
                [
                    gated[zhi, c, j, h, rows]
                    for j in range(NY) for c in range(2) for h in range(HALVES)
                ],
                axis=1,
            )
            right = jnp.concatenate([weights[zhi * 16 + j] for j in range(16)], axis=0)
            total[rows] = jnp.dot(left, right, preferred_element_type=F32)
            return carry

        lax.fori_loop(0, ROWS // 256, rows_of, 0)

    def far_product(h, n):
        part = gated.at[other, 1 - core, :, h, pl.ds(n * PIECE, PIECE)]
        arrived(part, c_recv.at[1, h, n])
        rows = pl.ds(n * PIECE, PIECE)
        pairs = [(j, c) for j in range(NY) for c in range(2)]
        left = jnp.concatenate([gated[other, c, j, h, rows] for j, c in pairs], axis=1)
        right = jnp.concatenate(
            [weights[other * 16 + j * 4 + c * 2 + h] for j, c in pairs], axis=0
        )
        summed = total[rows] + jnp.dot(left, right, preferred_element_type=F32)
        if h == HALVES - 1:
            out_ref[rows] = summed.astype(BF16)
        else:
            total[rows] = summed

    order = [(h, n) for h in range(HALVES) for n in range(PIECES)]
    near_at = 3
    for s in range(len(order) + 2):
        if s < len(order):
            pass_on(*order[s])
        if s == near_at:
            near_product()
            for t in range(s - 1):
                far_product(*order[t])
        if 1 <= s <= len(order):
            pass_core(*order[s - 1])
        if s > near_at:
            far_product(*order[s - 2])

    for c in sends + round_x + round_z + round_p:
        c.wait_send()
    for n in range(len(HOPS)):
        @pl.when(w_right(n))
        def _():
            w_copy_z(n, True).wait_send()

        @pl.when(w_left(n))
        def _():
            w_copy_z(n, False).wait_send()

    for z in range(NZ):
        for i in range(1, NX):
            w_copy_x(z, i).wait_send()


def body(
    query_in, key_in, value_in, residue, decay_rate, frequency, skip_gain, out_weight, cotangent
):
    def arranged(array):
        return array.reshape(HALVES, LANES, GROUPS, PER).transpose(0, 2, 3, 1)

    decay, freq = arranged(decay_rate), arranged(frequency)
    count = jnp.array([1.0, STEP, STRETCH, ROWS, ROWS * NX], F32).reshape(5, 1, 1)
    size = jnp.exp(-(decay[:, :, None] * count))
    angle = freq[:, :, None] * count
    table = jnp.concatenate([size * jnp.cos(angle), size * jnp.sin(angle)], axis=3)
    gain = jnp.concatenate([arranged(residue)] * 2, axis=2)[:, :, None]
    params = jnp.concatenate([table, gain], axis=2)

    vmem = pl.BlockSpec(memory_space=pltpu.VMEM)
    stream = jax.ShapeDtypeStruct((ROWS, HALVES * LANES), BF16)
    hbm = pl.BlockSpec(memory_space=pl.ANY)
    sem = pltpu.SemaphoreType.DMA
    tile = (SUBS, LANES)
    return pl.pallas_call(
        kernel,
        out_shape=(stream,) * 4,
        in_specs=[hbm] * 5 + [vmem] * 2,
        out_specs=(vmem,) * 4,
        scratch_shapes=[
            *[pltpu.VMEM((ROWS, HALVES * LANES), BF16)] * 4,
            pltpu.VMEM((HALVES, ROWS, LANES), F32),
            pltpu.VMEM((HALVES, ROWS, LANES), F32),
            pltpu.VMEM((HALVES, ROWS, LANES), F32),
            pltpu.VMEM((2, HALVES, STEP, LOS) + tile, F32),
            pltpu.VMEM((2, HALVES, GROUPS, 2 * PER, LOS) + tile, F32),
            pltpu.VMEM((2, HALVES, GROUPS, 2 * PER) + tile, F32),
            pltpu.VMEM((GROUPS, 2 * PER, LOS) + tile, F32),
            pltpu.VMEM((HALVES, GROUPS, STEP + 1, 2 * PER, LANES), F32),
            pltpu.VMEM((HALVES, STEP, LANES), F32),
            pltpu.VMEM((2, HALVES, GROUPS, 2 * PER) + tile, F32),
            pltpu.VMEM((GROUPS, HALVES, 4 * PER, LANES), F32),
            pltpu.VMEM((NX, HALVES, 4 * PER, LANES), F32),
            pltpu.VMEM((2, HALVES, 2 * PER, LANES), F32),
            pltpu.VMEM((NZ, HALVES, 2 * PER, LANES), F32),
            pltpu.VMEM((NX, HALVES, 4 * PER, LANES), F32),
            pltpu.VMEM((GROUPS, HALVES, 4 * PER, LANES), F32),
            pltpu.VMEM((NZ * NX, 128, HALVES * LANES), BF16),
            pltpu.VMEM((2, 2, NY, HALVES, ROWS, LANES), BF16),
            pltpu.VMEM((ROWS, HALVES * LANES), F32),
            sem((5,)),
            sem((2, len(HOPS))),
            sem((NZ, NX)),
            sem((NZ * NX,)),
            sem((3, NZ)),
            sem((NX,)),
            sem((NZ,)),
            sem((NX,)),
            sem((HALVES, PIECES + 4)),
            sem((1 + PIECES, HALVES, 4)),
            sem((2, NY, HALVES, PIECES)),
            sem((2, HALVES, PIECES)),
        ],
        compiler_params=pltpu.CompilerParams(
            collective_id=0, has_side_effects=True, vmem_limit_bytes=48 * 1024 * 1024
        ),
    )(query_in, key_in, value_in, cotangent, out_weight, params, skip_gain.reshape(1, -1))


def solution(mesh):
    return jax.shard_map(
        body,
        mesh=mesh,
        in_specs=(
            P("ctx", "tp"),
            P("ctx", "tp"),
            P("ctx", "tp"),
            P("tp", None),
            P("tp", None),
            P("tp", None),
            P("tp"),
            P("ctx", "tp"),
            P("ctx", "tp"),
        ),
        out_specs=(P("ctx", "tp"), P("ctx", "tp"), P("ctx", "tp"), P("ctx", "tp")),
        check_vma=False,
    )
```

```python
import jax
import jax.numpy as jnp
from jax import lax
from jax.experimental import pallas as pl
from jax.experimental.pallas import tpu as pltpu
from jax.sharding import PartitionSpec as P

F32 = jnp.float32
BF16 = jnp.bfloat16
MESH = pl.DeviceIdType.MESH

NZ, NX, NY = 8, 4, 4
ROWS, LANES, HALVES = 512, 128, 2
STEP, LOS, SUBS = 16, 4, 8
STRETCH = STEP * LOS
GROUPS, PER = 4, 4
PIECES = 2
PIECE = ROWS // PIECES
HOPS = ((0, 1), (0, 4), (1, 1), (2, 1), (4, 1), (4, 2), (4, 3))
FIRST, CHUNK, WIDE, DEVICE, COLUMN, GAIN = range(6)


def cmul(ar, ai, br, bi):
    return ar * br - ai * bi, ar * bi + ai * br


def shifted(value, amount, back):
    row = lax.broadcasted_iota(jnp.int32, (SUBS, LANES), 0)
    if back:
        return jnp.where(row < SUBS - amount, pltpu.roll(value, SUBS - amount, 0), 0.0)
    return jnp.where(row >= amount, pltpu.roll(value, amount, 0), 0.0)


def kernel(
    q_hbm,
    k_hbm,
    v_hbm,
    g_hbm,
    w_hbm,
    par_ref,
    skip_ref,
    out_ref,
    gq_ref,
    gk_ref,
    gv_ref,
    q_ref,
    k_ref,
    v_ref,
    g_ref,
    mixed,
    grad_in,
    conv,
    partial,
    chunk_state,
    entry,
    zstate,
    powers,
    taps,
    wide_pow,
    own_state,
    recv_x,
    column,
    recv_z,
    prefix,
    entry_in,
    weights,
    gated,
    total,
    in_sem,
    w_send_z,
    w_send_x,
    w_recv,
    s_send,
    x_recv,
    z_recv,
    p_recv,
    g_send,
    f_send,
    g_recv,
    c_recv,
):
    ctx = lax.axis_index("ctx")
    tp = lax.axis_index("tp")
    zlo, x = lax.div(ctx, NX), lax.rem(ctx, NX)
    zhi, y, core = lax.div(tp, 2 * NY), lax.rem(lax.div(tp, 2), NY), lax.rem(tp, 2)

    loads = [
        pltpu.make_async_copy(src, dst, in_sem.at[n])
        for n, (src, dst) in enumerate(
            [(k_hbm, k_ref), (v_hbm, v_ref), (q_hbm, q_ref), (g_hbm, g_ref)]
            + [(w_hbm, weights.at[ctx])]
        )
    ]
    for load in loads:
        load.start()

    def at_x(step):
        return (zlo * NX + lax.rem(x + step, NX), tp)

    def at_z(step):
        return (lax.rem(zlo + step, NZ) * NX + x, tp)

    def tp_of(h, yy, c):
        return (h * NY + yy) * 2 + c

    def at_y(step):
        return (ctx, tp_of(zhi, lax.rem(y + step, NY), core))

    far = (ctx, tp_of(1 - zhi, y, core))
    sibling = (ctx, tp_of(zhi, y, 1 - core))

    barrier = pltpu.get_barrier_semaphore()
    partners = [at_x(i) for i in range(1, NX)] + [at_z(i) for i in range(1, NZ)]
    partners += [at_y(i) for i in range(1, NY)] + [far, sibling]
    for partner in partners:
        pl.semaphore_signal(barrier, inc=1, device_id=partner, device_id_type=MESH)

    def copy(src, dst, send, recv, device):
        return pltpu.make_async_remote_copy(
            src_ref=src, dst_ref=dst, send_sem=send, recv_sem=recv,
            device_id=device, device_id_type=MESH,
        )

    def w_copy_z(n, right):
        away, hop = HOPS[n]
        block = (zlo - away if right else zlo + away) * NX + x
        slot = weights.at[block]
        to = (ctx + hop * NX, tp) if right else (ctx - hop * NX, tp)
        return copy(slot, slot, w_send_z.at[0 if right else 1, n], w_recv.at[block], to)

    def w_copy_x(z, step):
        block = z * NX + x
        slot = weights.at[block]
        return copy(slot, slot, w_send_x.at[z, step], w_recv.at[block], at_x(step))

    def w_wait_recv(block):
        slot = weights.at[block]
        copy(slot, slot, w_send_x.at[0, 0], w_recv.at[block], at_x(1)).wait_recv()

    def w_right(n):
        away, hop = HOPS[n]
        return jnp.logical_and(zlo - away >= 0, zlo + hop < NZ)

    def w_left(n):
        away, hop = HOPS[n]
        return jnp.logical_and(zlo + away < NZ, zlo - hop >= 0)

    def w_arrived(step):
        @pl.when(zlo - step >= 0)
        def _():
            w_wait_recv((zlo - step) * NX + x)

        @pl.when(zlo + step < NZ)
        def _():
            w_wait_recv((zlo + step) * NX + x)

    def w_step(*which):
        for n in which:
            @pl.when(w_right(n))
            def _():
                w_copy_z(n, True).start()

            @pl.when(w_left(n))
            def _():
                w_copy_z(n, False).start()

    def w_spread(step):
        @pl.when(zlo - step >= 0)
        def _():
            for i in range(1, NX):
                w_copy_x(zlo - step, i).start()

        if step:
            @pl.when(zlo + step < NZ)
            def _():
                for i in range(1, NX):
                    w_copy_x(zlo + step, i).start()

    def make_tables(h):
        def group(mg, acc):
            one = par_ref[h, mg, FIRST]
            ar, ai = one[:PER], one[PER:]
            gain = par_ref[h, mg, GAIN][:PER]
            pr, pi = jnp.ones_like(ar), jnp.zeros_like(ai)
            acc = list(acc)
            for p in range(STEP + 1):
                powers[h, mg, p] = jnp.concatenate([pr, pi], axis=0)
                if p < STEP:
                    acc[p] = acc[p] + gain * pr
                    pr, pi = cmul(pr, pi, ar, ai)
            return tuple(acc)

        acc = lax.fori_loop(0, GROUPS, group, (jnp.zeros((PER, LANES), F32),) * STEP)
        for p in range(STEP):
            taps[h, pl.ds(p, 1)] = jnp.sum(acc[p], axis=0, keepdims=True)

    def make_wide(index, carry):
        h, mg = lax.div(index, GROUPS), lax.rem(index, GROUPS)
        row = lax.broadcasted_iota(jnp.int32, (SUBS, LANES), 0)
        for back in (False, True):
            for i in range(PER):
                start = jnp.where(row == (SUBS - 1 if back else 0), 1.0, 0.0).astype(F32)
                re, im = scan_wide(h, mg, i, start, jnp.zeros_like(start), back)
                wide_pow[int(back), h, mg, i] = re
                wide_pow[int(back), h, mg, PER + i] = im
        return carry

    def scan_wide(h, mg, i, re, im, back):
        br = par_ref[h, mg, WIDE, pl.ds(i, 1)]
        bi = par_ref[h, mg, WIDE, pl.ds(PER + i, 1)]
        for amount in (1, 2, 4):
            sr, si = cmul(br, bi, shifted(re, amount, back), shifted(im, amount, back))
            re, im = re + sr, im + si
            if amount < 4:
                br, bi = cmul(br, bi, br, bi)
        return re, im

    def rows_at(lo, b):
        return pl.ds(lo * STEP + b, SUBS, stride=STRETCH)

    def state_in(back, signal, index):
        h, mg = lax.div(index, GROUPS), lax.rem(index, GROUPS)
        way = int(back)
        acc = [[None] * LOS for _ in range(2 * PER)]
        for p in range(STEP):
            b = p if back else STEP - 1 - p
            values = [signal[h, rows_at(lo, b)] for lo in range(LOS)]
            for r in range(2 * PER):
                if p == 0:
                    for lo in range(LOS):
                        acc[r][lo] = values[lo] if r < PER else jnp.zeros_like(values[lo])
                    continue
                coef = powers[h, mg, p, pl.ds(r, 1)]
                for lo in range(LOS):
                    acc[r][lo] = acc[r][lo] + coef * values[lo]
        for i in range(PER):
            cr = par_ref[h, mg, CHUNK, pl.ds(i, 1)]
            ci = par_ref[h, mg, CHUNK, pl.ds(PER + i, 1)]
            order = list(range(LOS))[::-1] if back else list(range(LOS))
            ur, ui = acc[i][order[0]], acc[PER + i][order[0]]
            for lo in order[1:]:
                ur, ui = cmul(cr, ci, ur, ui)
                ur, ui = ur + acc[i][lo], ui + acc[PER + i][lo]
            for lo in range(LOS):
                chunk_state[way, h, mg, i, lo] = acc[i][lo]
                chunk_state[way, h, mg, PER + i, lo] = acc[PER + i][lo]
            er, ei = scan_wide(h, mg, i, shifted(ur, 1, back), shifted(ui, 1, back), back)
            entry[way, h, mg, i] = er
            entry[way, h, mg, PER + i] = ei
            br = par_ref[h, mg, WIDE, pl.ds(i, 1)]
            bi = par_ref[h, mg, WIDE, pl.ds(PER + i, 1)]
            dr, di = cmul(br, bi, er, ei)
            last = 0 if back else SUBS - 1
            own_state[mg, h, pl.ds(way * 8 + i, 1)] = (dr + ur)[last : last + 1]
            own_state[mg, h, pl.ds(way * 8 + PER + i, 1)] = (di + ui)[last : last + 1]

    def inside(back, signal, h):
        coef = [taps[h, pl.ds(p, 1)] for p in range(STEP)]
        for lo in range(LOS):
            values = [signal[h, rows_at(lo, b)] for b in range(STEP)]
            for b in range(STEP):
                js = range(b, STEP) if back else range(b + 1)
                acc = None
                for j in js:
                    term = coef[abs(b - j)] * values[j]
                    acc = term if acc is None else acc + term
                partial[int(back), h, b, lo] = acc

    def inject(back, h):
        way = int(back)

        def prepare(mg, carry):
            for i in range(PER):
                pr = entry_in[mg, h, pl.ds(way * 8 + i, 1)]
                pi = entry_in[mg, h, pl.ds(way * 8 + PER + i, 1)]
                er, ei = cmul(wide_pow[way, h, mg, i], wide_pow[way, h, mg, PER + i], pr, pi)
                zr, zi = er + entry[way, h, mg, i], ei + entry[way, h, mg, PER + i]
                cr = par_ref[h, mg, CHUNK, pl.ds(i, 1)]
                ci = par_ref[h, mg, CHUNK, pl.ds(PER + i, 1)]
                gain = par_ref[h, mg, GAIN, pl.ds(i, 1)]
                order = list(range(LOS))[::-1] if back else list(range(LOS))
                for n, lo in enumerate(order):
                    zstate[mg, i, lo] = gain * zr
                    zstate[mg, PER + i, lo] = -(gain * zi)
                    if n < LOS - 1:
                        zr, zi = cmul(cr, ci, zr, zi)
                        zr = zr + chunk_state[way, h, mg, i, lo]
                        zi = zi + chunk_state[way, h, mg, PER + i, lo]
            return carry

        lax.fori_loop(0, GROUPS, prepare, 0)
        for b0 in range(0, STEP, 4):

            def group(mg, acc):
                acc = list(acc)
                for r in range(2 * PER):
                    states = [zstate[mg, r, lo] for lo in range(LOS)]
                    for n in range(4):
                        b = b0 + n
                        coef = powers[h, mg, STEP - b if back else b + 1, pl.ds(r, 1)]
                        for lo in range(LOS):
                            acc[n * LOS + lo] = acc[n * LOS + lo] + coef * states[lo]
                return tuple(acc)

            start = tuple(partial[way, h, b0 + n, lo] for n in range(4) for lo in range(LOS))
            acc = lax.fori_loop(0, GROUPS, group, start)
            for n in range(4):
                for lo in range(LOS):
                    conv[h, rows_at(lo, b0 + n)] = acc[n * LOS + lo]

    def lanes(h):
        return pl.ds(h * LANES, LANES)

    def prepare_rows(h):
        for r0 in range(0, ROWS, 128):
            rows = pl.ds(r0, 128)
            prod = k_ref[rows, lanes(h)].astype(F32) * v_ref[rows, lanes(h)].astype(F32)
            mixed[h, rows] = prod.astype(BF16).astype(F32)
            prod = g_ref[rows, lanes(h)].astype(F32) * q_ref[rows, lanes(h)].astype(F32)
            grad_in[h, rows] = prod.astype(BF16).astype(F32)

    def gate_forward(h):
        skip = skip_ref[:, lanes(h)]
        for r0 in range(0, ROWS, 128):
            rows = pl.ds(r0, 128)
            summed = conv[h, rows].astype(BF16).astype(F32) + skip * mixed[h, rows]
            gated[zhi, core, y, h, rows] = (q_ref[rows, lanes(h)].astype(F32) * summed).astype(BF16)
            gq_ref[rows, lanes(h)] = (g_ref[rows, lanes(h)].astype(F32) * summed).astype(BF16)

    def gate_backward(h):
        skip = skip_ref[:, lanes(h)]
        for r0 in range(0, ROWS, 128):
            rows = pl.ds(r0, 128)
            summed = conv[h, rows].astype(BF16).astype(F32) + skip * grad_in[h, rows]
            gk_ref[rows, lanes(h)] = (summed * v_ref[rows, lanes(h)].astype(F32)).astype(BF16)
            gv_ref[rows, lanes(h)] = (summed * k_ref[rows, lanes(h)].astype(F32)).astype(BF16)

    for h in range(HALVES):
        make_tables(h)
    for load in loads[:-1]:
        load.wait()
    for h in range(HALVES):
        prepare_rows(h)

    def forward_states(index, carry):
        state_in(False, mixed, index)
        return carry

    def backward_states(index, carry):
        state_in(True, grad_in, index)
        return carry

    lax.fori_loop(0, HALVES * GROUPS, forward_states, 0)
    lax.fori_loop(0, HALVES * GROUPS, backward_states, 0)
    loads[-1].wait()
    pl.semaphore_wait(barrier, len(partners))

    round_x = [
        copy(own_state.at[lax.rem(x + i, NX)], recv_x.at[x], s_send.at[0, i], x_recv.at[x], at_x(i))
        for i in range(1, NX)
    ]
    for c in round_x:
        c.start()
    recv_x[x] = own_state[x]
    w_step(0, 1)
    for h in range(HALVES):
        inside(False, mixed, h)
    for i in range(1, NX):
        src = lax.rem(x + NX - i, NX)
        copy(own_state.at[0], recv_x.at[src], s_send.at[0, i], x_recv.at[src], at_x(i)).wait_recv()

    def cpack(value):
        return value[:PER], value[PER:]

    def step_on(power, h, state, added):
        re, im = cmul(*cpack(par_ref[h, x, power]), *cpack(state))
        return jnp.concatenate([re, im], axis=0) + added

    for h in range(HALVES):
        state = recv_x[0, h, pl.ds(0, 8)]
        for i in range(1, NX):
            state = step_on(DEVICE, h, state, recv_x[i, h, pl.ds(0, 8)])
        column[0, h] = state
        state = recv_x[NX - 1, h, pl.ds(8, 8)]
        for i in range(NX - 2, -1, -1):
            state = step_on(DEVICE, h, state, recv_x[i, h, pl.ds(8, 8)])
        column[1, h] = state

    round_z = []
    for i in range(1, NZ):
        way = jnp.where(zlo + i < NZ, 0, 1)
        round_z.append(
            copy(column.at[way], recv_z.at[zlo], s_send.at[1, i], z_recv.at[zlo], at_z(i))
        )
    for c in round_z:
        c.start()
    recv_z[zlo] = jnp.zeros_like(recv_z[zlo])
    w_spread(0)
    w_arrived(1)
    w_step(2)
    w_arrived(4)
    w_step(4, 5, 6)
    lax.fori_loop(0, HALVES * GROUPS, make_wide, 0)
    for h in range(HALVES):
        inside(True, grad_in, h)
    for i in range(1, NZ):
        src = lax.rem(zlo + NZ - i, NZ)
        copy(column.at[0], recv_z.at[src], s_send.at[1, i], z_recv.at[src], at_z(i)).wait_recv()

    for h in range(HALVES):
        state = jnp.zeros((2 * PER, LANES), F32)
        for z in range(NZ):
            state = jnp.where(z < zlo, step_on(COLUMN, h, state, recv_z[z, h]), state)
        for i in range(NX):
            prefix[i, h, pl.ds(0, 8)] = state
            if i < NX - 1:
                state = step_on(DEVICE, h, state, recv_x[i, h, pl.ds(0, 8)])
        state = jnp.zeros((2 * PER, LANES), F32)
        for z in range(NZ - 1, -1, -1):
            state = jnp.where(z > zlo, step_on(COLUMN, h, state, recv_z[z, h]), state)
        for i in range(NX - 1, -1, -1):
            prefix[i, h, pl.ds(8, 8)] = state
            if i > 0:
                state = step_on(DEVICE, h, state, recv_x[i, h, pl.ds(8, 8)])

    round_p = [
        copy(prefix.at[lax.rem(x + i, NX)], entry_in.at[x], s_send.at[2, i], p_recv.at[x], at_x(i))
        for i in range(1, NX)
    ]
    for c in round_p:
        c.start()
    entry_in[x] = prefix[x]
    w_arrived(2)
    w_step(3)
    for i in range(1, NX):
        src = lax.rem(x + NX - i, NX)
        copy(prefix.at[0], entry_in.at[src], s_send.at[2, i], p_recv.at[src], at_x(i)).wait_recv()

    def piece(side, yy, h, n):
        return gated.at[side, core, yy, h, pl.ds(n * PIECE, PIECE)]

    def half(side, yy, h):
        return gated.at[side, core, yy, h]

    sends = []

    def send(src, sem, recv, to):
        c = copy(src, src, sem, recv, to)
        c.start()
        sends.append(c)

    def send_far(h, n):
        send(piece(zhi, y, h, n), g_send.at[h, n], g_recv.at[zhi, y, h, n], far)

    for h in range(HALVES):
        inject(False, h)
        gate_forward(h)
        for n in range(PIECES):
            send_far(h, n)
        for i in range(1, NY):
            send(half(zhi, y, h), g_send.at[h, PIECES + i - 1], g_recv.at[zhi, y, h, 0], at_y(i))
        w_spread(1 + h)

    for h in range(HALVES):
        inject(True, h)
        gate_backward(h)
        w_spread(4 - h)
        if h == 0:
            w_arrived(3)
    for step in range(5, NZ):
        w_arrived(step)
        w_spread(step)

    other = 1 - zhi

    def arrived(part, recv):
        copy(part, part, g_send.at[0, 0], recv, far).wait_recv()

    for h in range(HALVES):
        for i in range(1, NY):
            yy = lax.rem(y + i, NY)
            arrived(half(zhi, yy, h), g_recv.at[zhi, yy, h, 0])
        send(gated.at[zhi, core, :, h], f_send.at[0, h, 0], c_recv.at[0, h, 0], sibling)

    def pass_on(h, n):
        part = piece(other, y, h, n)
        arrived(part, g_recv.at[other, y, h, n])
        for i in range(1, NY):
            send(part, f_send.at[1 + n, h, i], g_recv.at[other, y, h, n], at_y(i))

    def along_y(h, n):
        return gated.at[other, core, :, h, pl.ds(n * PIECE, PIECE)]

    def pass_core(h, n):
        for i in range(1, NY):
            yy = lax.rem(y + i, NY)
            arrived(piece(other, yy, h, n), g_recv.at[other, yy, h, n])
        send(along_y(h, n), f_send.at[1 + n, h, 0], c_recv.at[1, h, n], sibling)

    def w_rows(side):
        for z in range(NZ // 2):
            for i in range(1, NX):
                w_wait_recv((side * (NZ // 2) + z) * NX + lax.rem(x + i, NX))

    def near_product():
        for h in range(HALVES):
            arrived(gated.at[zhi, 1 - core, :, h], c_recv.at[0, h, 0])

        w_rows(zhi)

        def rows_of(n, carry):
            rows = pl.ds(pl.multiple_of(n * 256, 256), 256)
            left = jnp.concatenate(
                [
                    gated[zhi, c, j, h, rows]
                    for j in range(NY) for c in range(2) for h in range(HALVES)
                ],
                axis=1,
            )
            right = jnp.concatenate([weights[zhi * 16 + j] for j in range(16)], axis=0)
            total[rows] = jnp.dot(left, right, preferred_element_type=F32)
            return carry

        lax.fori_loop(0, ROWS // 256, rows_of, 0)

    def far_product(h, n):
        part = gated.at[other, 1 - core, :, h, pl.ds(n * PIECE, PIECE)]
        arrived(part, c_recv.at[1, h, n])
        rows = pl.ds(n * PIECE, PIECE)
        pairs = [(j, c) for j in range(NY) for c in range(2)]
        left = jnp.concatenate([gated[other, c, j, h, rows] for j, c in pairs], axis=1)
        right = jnp.concatenate(
            [weights[other * 16 + j * 4 + c * 2 + h] for j, c in pairs], axis=0
        )
        summed = total[rows] + jnp.dot(left, right, preferred_element_type=F32)
        if h == HALVES - 1:
            out_ref[rows] = summed.astype(BF16)
        else:
            total[rows] = summed

    order = [(h, n) for h in range(HALVES) for n in range(PIECES)]
    near_at = 1
    for s in range(len(order) + 2):
        if s < len(order):
            pass_on(*order[s])
        if s == near_at:
            near_product()
            w_rows(other)
        if 1 <= s <= len(order):
            pass_core(*order[s - 1])
        if s == near_at:
            for t in range(max(s - 1, 0)):
                far_product(*order[t])
        elif s > near_at and s >= 2:
            far_product(*order[s - 2])

    for c in sends + round_x + round_z + round_p:
        c.wait_send()
    for n in range(len(HOPS)):
        @pl.when(w_right(n))
        def _():
            w_copy_z(n, True).wait_send()

        @pl.when(w_left(n))
        def _():
            w_copy_z(n, False).wait_send()

    for z in range(NZ):
        for i in range(1, NX):
            w_copy_x(z, i).wait_send()


def body(
    query_in, key_in, value_in, residue, decay_rate, frequency, skip_gain, out_weight, cotangent
):
    def arranged(array):
        return array.reshape(HALVES, LANES, GROUPS, PER).transpose(0, 2, 3, 1)

    decay, freq = arranged(decay_rate), arranged(frequency)
    count = jnp.array([1.0, STEP, STRETCH, ROWS, ROWS * NX], F32).reshape(5, 1, 1)
    size = jnp.exp(-(decay[:, :, None] * count))
    angle = freq[:, :, None] * count
    table = jnp.concatenate([size * jnp.cos(angle), size * jnp.sin(angle)], axis=3)
    gain = jnp.concatenate([arranged(residue)] * 2, axis=2)[:, :, None]
    params = jnp.concatenate([table, gain], axis=2)

    vmem = pl.BlockSpec(memory_space=pltpu.VMEM)
    stream = jax.ShapeDtypeStruct((ROWS, HALVES * LANES), BF16)
    hbm = pl.BlockSpec(memory_space=pl.ANY)
    sem = pltpu.SemaphoreType.DMA
    tile = (SUBS, LANES)
    return pl.pallas_call(
        kernel,
        out_shape=(stream,) * 4,
        in_specs=[hbm] * 5 + [vmem] * 2,
        out_specs=(vmem,) * 4,
        scratch_shapes=[
            *[pltpu.VMEM((ROWS, HALVES * LANES), BF16)] * 4,
            pltpu.VMEM((HALVES, ROWS, LANES), F32),
            pltpu.VMEM((HALVES, ROWS, LANES), F32),
            pltpu.VMEM((HALVES, ROWS, LANES), F32),
            pltpu.VMEM((2, HALVES, STEP, LOS) + tile, F32),
            pltpu.VMEM((2, HALVES, GROUPS, 2 * PER, LOS) + tile, F32),
            pltpu.VMEM((2, HALVES, GROUPS, 2 * PER) + tile, F32),
            pltpu.VMEM((GROUPS, 2 * PER, LOS) + tile, F32),
            pltpu.VMEM((HALVES, GROUPS, STEP + 1, 2 * PER, LANES), F32),
            pltpu.VMEM((HALVES, STEP, LANES), F32),
            pltpu.VMEM((2, HALVES, GROUPS, 2 * PER) + tile, F32),
            pltpu.VMEM((GROUPS, HALVES, 4 * PER, LANES), F32),
            pltpu.VMEM((NX, HALVES, 4 * PER, LANES), F32),
            pltpu.VMEM((2, HALVES, 2 * PER, LANES), F32),
            pltpu.VMEM((NZ, HALVES, 2 * PER, LANES), F32),
            pltpu.VMEM((NX, HALVES, 4 * PER, LANES), F32),
            pltpu.VMEM((GROUPS, HALVES, 4 * PER, LANES), F32),
            pltpu.VMEM((NZ * NX, 128, HALVES * LANES), BF16),
            pltpu.VMEM((2, 2, NY, HALVES, ROWS, LANES), BF16),
            pltpu.VMEM((ROWS, HALVES * LANES), F32),
            sem((5,)),
            sem((2, len(HOPS))),
            sem((NZ, NX)),
            sem((NZ * NX,)),
            sem((3, NZ)),
            sem((NX,)),
            sem((NZ,)),
            sem((NX,)),
            sem((HALVES, PIECES + 4)),
            sem((1 + PIECES, HALVES, 4)),
            sem((2, NY, HALVES, PIECES)),
            sem((2, HALVES, PIECES)),
        ],
        compiler_params=pltpu.CompilerParams(
            collective_id=0, has_side_effects=True, vmem_limit_bytes=48 * 1024 * 1024
        ),
    )(query_in, key_in, value_in, cotangent, out_weight, params, skip_gain.reshape(1, -1))


def solution(mesh):
    return jax.shard_map(
        body,
        mesh=mesh,
        in_specs=(
            P("ctx", "tp"),
            P("ctx", "tp"),
            P("ctx", "tp"),
            P("tp", None),
            P("tp", None),
            P("tp", None),
            P("tp"),
            P("ctx", "tp"),
            P("ctx", "tp"),
        ),
        out_specs=(P("ctx", "tp"), P("ctx", "tp"), P("ctx", "tp"), P("ctx", "tp")),
        check_vma=False,
    )
```
